512 devices in a mesh: seq: 64 (over z, x, core), tp: 8 (over y).
Axes of the slice: x: 4, y: 8, z: 8, core: 2. Of those that a mesh axis runs over, the one named last changes fastest.
Arguments:
- query_beam: bfloat16 [32768, 5120], P(('seq', 'tp')), may hold values from -6 to 6
- key_value_beam: bfloat16 [32768, 2048], P(('seq', 'tp')), may hold values from -24 to 24, as said below
- beam_row_index: int32 [32768], replicated, may hold values from 0 to 32767, as said below
- ancestors: int32 [256, 10], P('seq'), may hold values from 0 to 255, as said below
- depth: int32 [256], P('seq'), may hold values from 0 to 10, as said below
Outputs:
- attended: bfloat16 [32768, 5120], P('seq', 'tp')
The draws below stay inside these ranges and needn't reach their ends.
Inputs may be any that keep to these rules, and one draw needn't show every extreme that they name: A permutation of the packed rows: beam_row_index[p] is the beam row that lands at packed row p. Each beam device, holding 64 rows, holds exactly 1 row of each packed shard of 512 rows. For j < depth[g], ancestors[g, j] is the block at depth j on the path from the root of g's tree to g, an earlier block; the slots from depth[g] on hold g itself. A tree is 32 consecutive blocks, and its first 3 blocks form a chain. `depth`: the number of ancestors of each block. `key_value_beam`: keys lie within -5 to 5.
All inputs are finite; a program needn't handle non-finite values.
Results may differ from the reference program's by a relative error of at most 0.0048.
Values may be sent and summed in bfloat16 or wider, within the bound.
No kernel may reach another device: no remote copies, remote signals or barrier semaphores. Data moves between devices by JAX's collectives and lax.ppermute only.
A program may use at most 64 MiB of HBM per device.

```python
import math
import jax
import jax.numpy as jnp
from jax import lax

QUERY_HEADS = 40
KEY_VALUE_HEADS = 8
HEAD_WIDTH = 128
BLOCK_TOKENS = 128
ANCESTOR_SLOTS = 10
PROMPT_BLK = 3
TREE_SHARDS = 8
TOK_DEV = 512
TOKEN_COUNT = 32768
BLOCK_COUNT = 256
TREE_BLK = 32
BEAM_DEV = 64
ROWS_PEER = 1
N_SEQ = 64
N_TP = 8


def packed_map(key):
    key = jax.random.fold_in(key, 101)
    shard_keys = jax.random.split(jax.random.fold_in(key, 1), N_SEQ)
    dealt_slots = jax.vmap(lambda single: jax.random.permutation(single, TOK_DEV))(shard_keys).astype(jnp.int32)
    owner_keys = jax.random.split(jax.random.fold_in(key, 2), N_SEQ * N_TP)
    placed = jax.vmap(lambda single: jax.random.permutation(single, BEAM_DEV))(owner_keys).astype(jnp.int32)
    owners = dealt_slots // ROWS_PEER
    within = dealt_slots % ROWS_PEER
    shard_ids = jnp.arange(N_SEQ, dtype=jnp.int32)[:, None]
    column = shard_ids * ROWS_PEER + within
    local_row = placed[owners, column]
    return (owners * BEAM_DEV + local_row).reshape(TOKEN_COUNT).astype(jnp.int32)


def grow_trees(key):
    key = jax.random.fold_in(key, 202)
    tree_count = N_SEQ // TREE_SHARDS
    picked = jax.random.randint(jax.random.fold_in(key, 1), (tree_count, TREE_BLK), 0, 1 << 20, dtype=jnp.int32)
    forced = jax.random.randint(jax.random.fold_in(key, 2), (), 0, tree_count, dtype=jnp.int32)
    slot_ids = jnp.arange(ANCESTOR_SLOTS, dtype=jnp.int32)
    tree_ids = jnp.arange(tree_count, dtype=jnp.int32)
    parent = jnp.zeros((tree_count, TREE_BLK), jnp.int32)
    levels = jnp.zeros((tree_count, TREE_BLK), jnp.int32)
    path_index = jnp.zeros((tree_count, TREE_BLK, ANCESTOR_SLOTS), jnp.int32)

    def add_block(step, grown):
        parent, levels, path_index = grown
        lowest = PROMPT_BLK - 1
        chosen = lowest + picked[:, step] % jnp.maximum(step - lowest, 1)
        in_chain = (step < PROMPT_BLK) | (tree_ids == forced) & (step <= ANCESTOR_SLOTS)
        chosen = jnp.where(in_chain, step - 1, chosen).astype(jnp.int32)
        too_deep = levels[tree_ids, chosen] >= ANCESTOR_SLOTS
        chosen = jnp.where(too_deep, parent[tree_ids, chosen], chosen)
        parent_lvl = levels[tree_ids, chosen]
        inherited = path_index[tree_ids, chosen]
        new_path = jnp.where(slot_ids[None] < parent_lvl[:, None], inherited, jnp.where(slot_ids[None] == parent_lvl[:, None], chosen[:, None], step))
        return (parent.at[:, step].set(chosen), levels.at[:, step].set(parent_lvl + 1), path_index.at[:, step].set(new_path.astype(jnp.int32)))
    parent, levels, path_index = lax.fori_loop(1, TREE_BLK, add_block, (parent, levels, path_index))
    path_index = path_index + (tree_ids * TREE_BLK)[:, None, None]
    return (path_index.reshape(BLOCK_COUNT, ANCESTOR_SLOTS).astype(jnp.int32), levels.reshape(BLOCK_COUNT).astype(jnp.int32))


def draw_beam_row_index(key, part):
    return packed_map(key)


def draw_ancestors(key, part):
    return grow_trees(key)[0]


def draw_depth(key, part):
    return grow_trees(key)[1]


def draw_query_beam(key, part):
    own_key_rows = jax.random.fold_in(key, 11)
    drawn = jnp.clip(1.5 * jax.random.normal(own_key_rows, (TOKEN_COUNT, QUERY_HEADS * HEAD_WIDTH), jnp.float32), -6.0, 6.0)
    return drawn.astype(jnp.bfloat16)


def draw_key_value_beam(key, part):
    own_key_rows = jax.random.fold_in(key, 13)
    key_portion = jnp.clip(jax.random.normal(jax.random.fold_in(own_key_rows, 3), (TOKEN_COUNT, KEY_VALUE_HEADS, HEAD_WIDTH), jnp.float32), -5.0, 5.0)
    value_portion = jnp.clip(8.0 * jax.random.normal(jax.random.fold_in(own_key_rows, 4), (TOKEN_COUNT, KEY_VALUE_HEADS, HEAD_WIDTH), jnp.float32), -24.0, 24.0)
    joined_rows = jnp.stack([key_portion, value_portion], 2)
    return joined_rows.reshape(TOKEN_COUNT, KEY_VALUE_HEADS * 2 * HEAD_WIDTH).astype(jnp.bfloat16)


def setup_inputs(seed: int = 0) -> dict:
    seeds = jax.random.split(jax.random.key(seed), 6)
    return {
        "query_beam": draw_query_beam(jax.random.fold_in(seeds[5], 71), 0),
        "key_value_beam": draw_key_value_beam(jax.random.fold_in(seeds[5], 71), 0),
        "beam_row_index": draw_beam_row_index(jax.random.fold_in(seeds[5], 71), 0),
        "ancestors": draw_ancestors(jax.random.fold_in(seeds[5], 71), 0),
        "depth": draw_depth(jax.random.fold_in(seeds[5], 71), 0),
    }


def reference(query_beam, key_value_beam, beam_row_index, ancestors, depth):
    queries_per_group = QUERY_HEADS // KEY_VALUE_HEADS
    query_rows = query_beam[beam_row_index].reshape(BLOCK_COUNT, BLOCK_TOKENS, KEY_VALUE_HEADS, queries_per_group, HEAD_WIDTH)
    head_pairs = key_value_beam[beam_row_index].reshape(BLOCK_COUNT, BLOCK_TOKENS, KEY_VALUE_HEADS, 2, HEAD_WIDTH)
    slot_of = jnp.arange((ANCESTOR_SLOTS + 1) * BLOCK_TOKENS, dtype=jnp.int32) // BLOCK_TOKENS
    offset = jnp.arange((ANCESTOR_SLOTS + 1) * BLOCK_TOKENS, dtype=jnp.int32) - ANCESTOR_SLOTS * BLOCK_TOKENS
    query_pos = jnp.arange(BLOCK_TOKENS, dtype=jnp.int32)[:, None]
    inv_root = 1.0 / math.sqrt(HEAD_WIDTH)

    def attend(block_id):
        path_index = ancestors[block_id]
        levels = depth[block_id]
        distant_blocks = head_pairs[path_index].reshape(ANCESTOR_SLOTS * BLOCK_TOKENS, KEY_VALUE_HEADS, 2, HEAD_WIDTH)
        key_rows = jnp.concatenate([distant_blocks, head_pairs[block_id]], 0).astype(jnp.float32)
        query_blk = query_rows[block_id].astype(jnp.float32)
        scores = jnp.einsum('bkgd,nkd->kgbn', query_blk, key_rows[:, :, 0]) * inv_root
        allowed = jnp.where(slot_of[None] < ANCESTOR_SLOTS, slot_of[None] < levels, offset[None] <= query_pos)
        scores = jnp.where(allowed, scores, -jnp.inf)
        largest = lax.optimization_barrier(jnp.max(scores, -1, keepdims=True))
        shifted = jnp.exp(scores - largest)
        normalizer = lax.optimization_barrier(jnp.sum(shifted, -1, keepdims=True))
        weights = (shifted / normalizer).astype(jnp.bfloat16)
        result = jnp.einsum('kgbn,nkd->bkgd', weights.astype(jnp.float32), key_rows[:, :, 1])
        return result.astype(jnp.bfloat16)
    attended = lax.map(attend, jnp.arange(BLOCK_COUNT, dtype=jnp.int32))
    return attended.reshape(TOKEN_COUNT, QUERY_HEADS * HEAD_WIDTH)
```

```python
import functools
import math

import jax
import jax.numpy as jnp
from jax import lax
from jax.experimental import pallas as pl
from jax.experimental.pallas import tpu as pltpu
from jax.sharding import Mesh
from jax.sharding import PartitionSpec as P

HEAD = 128
BLOCK = 128
SLOTS = 10
GROUP = 5
KEYS = (SLOTS + 1) * BLOCK
NEG = -1e30
VMEM_LIMIT = 40 * 1024 * 1024
NT = (((1,), (1,)), ((), ()))


def prep_kernel(place, index, query, pairs, out):
    device = place[0]
    idx = index[...]
    mine = (idx >> 6) == device
    local = jnp.where(mine, (idx & 63).astype(jnp.float32), 0.0).astype(jnp.bfloat16)
    shard = lax.broadcasted_iota(jnp.int32, (64, 256), 0)
    row = lax.broadcasted_iota(jnp.int32, (64, 256), 1)
    group = jnp.where((row >> 2) == shard, 1.0, 0.0).astype(jnp.bfloat16)
    by_shard = jnp.dot(group, local, preferred_element_type=jnp.float32)
    source = jnp.sum(by_shard, 1, keepdims=True).astype(jnp.int32)
    lane = lax.broadcasted_iota(jnp.int32, (64, 64), 1)
    picker = jnp.where(source == lane, 1.0, 0.0).astype(jnp.bfloat16)
    for t in range(8):
        q = jnp.dot(picker, query[:, t * 640 : (t + 1) * 640], preferred_element_type=jnp.float32)
        kv = jnp.dot(picker, pairs[:, t * 256 : (t + 1) * 256], preferred_element_type=jnp.float32)
        for z in range(8):
            out[z * 8 + t, :, :640] = q[z * 8 : (z + 1) * 8].astype(jnp.bfloat16)
            out[z * 8 + t, :, 640:] = kv[z * 8 : (z + 1) * 8].astype(jnp.bfloat16)


def arrival(idx, x, c, own):
    source = idx >> 6
    tail = ((source >> 6) << 3) | (source & 7)
    src_x, src_c = (source >> 4) & 3, (source >> 3) & 1
    if own:
        return (((src_x << 1) | src_c) << 6) | tail
    return ((((src_c ^ c) << 2) | ((x - src_x) & 3)) << 6) | tail


def picker_of(pos_row):
    column = jnp.transpose(jnp.broadcast_to(pos_row.astype(jnp.float32), (128, 128)))
    parts = []
    for k in range(4):
        lane = (lax.broadcasted_iota(jnp.int32, (128, 128), 1) + k * 128).astype(jnp.float32)
        parts.append(jnp.where(column == lane, 1.0, 0.0).astype(jnp.bfloat16))
    return jnp.concatenate(parts, 1)


def attend_kernel(
    place, ancestors, depth, index, query, a0, a1, a2, a3, b0, b1, b2, b3, out,
    keys, values, local_q, kc, vc, scores, probs,
):
    z, x, c = place[1], place[2], place[3]
    in_tree = x * 2 + c
    slabs = (a0, a1, a2, a3, b0, b1, b2, b3)

    def place_shard(j, carry):
        raw = jnp.concatenate([s[j] for s in slabs], 0)
        for n in range(4):
            idx = index[pl.ds(z * 32 + j * 4 + n, 1), :]
            pick = picker_of(arrival(idx, x, c, False))
            got = jnp.dot(pick, raw, preferred_element_type=jnp.float32).astype(jnp.bfloat16)
            keys[j * 4 + n] = got[:, :128]
            values[j * 4 + n] = got[:, 128:]
        return carry

    lax.fori_loop(0, in_tree + 1, place_shard, 0)
    for n in range(4):
        idx = index[pl.ds(z * 32 + in_tree * 4 + n, 1), :]
        pick = picker_of(arrival(idx, x, c, True))
        got = jnp.dot(pick, query[...], preferred_element_type=jnp.float32).astype(jnp.bfloat16)
        for h in range(GROUP):
            local_q[n, h * 128 : (h + 1) * 128, :] = got[:, h * 128 : (h + 1) * 128]
    vc[:, 128:] = jnp.ones((KEYS, 128), jnp.bfloat16)
    factor = math.log2(math.e) / math.sqrt(HEAD)

    def attend(b, carry):
        levels = depth[b]
        for j in range(SLOTS):
            block = ancestors[b, j] - z * 32
            kc[j * 128 : (j + 1) * 128, :] = keys[block]
            vc[j * 128 : (j + 1) * 128, :128] = values[block]
        me = in_tree * 4 + b
        kc[SLOTS * 128 :, :] = keys[me]
        vc[SLOTS * 128 :, :128] = values[me]
        scores[...] = lax.dot_general(local_q[b], kc[...], NT, preferred_element_type=jnp.float32)
        slot = lax.broadcasted_iota(jnp.int32, (1, SLOTS * 128), 1) >> 7
        bias = jnp.where(slot < levels, 0.0, NEG)
        r = lax.broadcasted_iota(jnp.int32, (128, 128), 0)
        n = lax.broadcasted_iota(jnp.int32, (128, 128), 1)
        causal = jnp.where(n <= r, 0.0, NEG)
        for h in range(GROUP):
            rows = slice(h * 128, (h + 1) * 128)
            s0 = scores[rows, : SLOTS * 128] + bias
            s1 = scores[rows, SLOTS * 128 :] + causal
            top = jnp.maximum(jnp.max(s0, 1, keepdims=True), jnp.max(s1, 1, keepdims=True))
            probs[rows, : SLOTS * 128] = jnp.exp2((s0 - top) * factor).astype(jnp.bfloat16)
            probs[rows, SLOTS * 128 :] = jnp.exp2((s1 - top) * factor).astype(jnp.bfloat16)
        acc = jnp.dot(probs[...], vc[...], preferred_element_type=jnp.float32)
        res = (acc[:, :128] / acc[:, 128:]).astype(jnp.bfloat16)
        for h in range(GROUP):
            out[pl.ds(pl.multiple_of(b * 128, 128), 128), h * 128 : (h + 1) * 128] = res[h * 128 : (h + 1) * 128]
        return carry

    lax.fori_loop(0, 4, attend, 0)


SMEM = pl.BlockSpec(memory_space=pltpu.SMEM)
VMEM = pl.BlockSpec(memory_space=pltpu.VMEM)


def shift(block, axis, size, distance):
    return lax.ppermute(block, axis, [(i, (i + distance) % size) for i in range(size)])


def body(query_beam, key_value_beam, beam_row_index, ancestors, depth):
    z, x, c, t = (lax.axis_index(n) for n in ("z", "x", "c", "t"))
    device = ((z * 4 + x) * 2 + c) * 8 + t
    place = jnp.stack([device, z, x, c]).astype(jnp.int32)
    index = beam_row_index.reshape(256, 128)
    packed = pl.pallas_call(
        prep_kernel,
        out_shape=jax.ShapeDtypeStruct((64, 8, 896), jnp.bfloat16),
        in_specs=[SMEM, VMEM, VMEM, VMEM],
        out_specs=VMEM,
        compiler_params=pltpu.CompilerParams(vmem_limit_bytes=VMEM_LIMIT),
        name="sort_rows",
    )(place, index, query_beam, key_value_beam)
    landed = lax.all_to_all(packed, ("z", "t"), split_axis=0, concat_axis=0, tiled=True)
    own = landed[:, :, 640:].transpose(1, 0, 2)
    query_out = landed[:, :, :640].transpose(1, 0, 2)
    same = [own] + [shift(own, "x", 4, d) for d in (1, 2, 3)]
    other = [shift(s, "c", 2, 1) for s in same]
    query = lax.all_to_all(query_out, ("x", "c"), split_axis=0, concat_axis=0, tiled=True)
    return pl.pallas_call(
        attend_kernel,
        out_shape=jax.ShapeDtypeStruct((512, 640), jnp.bfloat16),
        in_specs=[SMEM] * 3 + [VMEM] * 10,
        out_specs=VMEM,
        scratch_shapes=[
            pltpu.VMEM((32, 128, 128), jnp.bfloat16),
            pltpu.VMEM((32, 128, 128), jnp.bfloat16),
            pltpu.VMEM((4, 640, 128), jnp.bfloat16),
            pltpu.VMEM((KEYS, 128), jnp.bfloat16),
            pltpu.VMEM((KEYS, 256), jnp.bfloat16),
            pltpu.VMEM((640, KEYS), jnp.float32),
            pltpu.VMEM((640, KEYS), jnp.bfloat16),
        ],
        compiler_params=pltpu.CompilerParams(vmem_limit_bytes=VMEM_LIMIT),
        name="tree_attention",
    )(place, ancestors, depth, index, query.reshape(512, 640), *same, *other)


def solution(mesh):
    fine = Mesh(mesh.devices.reshape(8, 4, 2, 8), ("z", "x", "c", "t"))
    every, shard = ("z", "x", "c", "t"), ("z", "x", "c")
    return jax.shard_map(
        body,
        mesh=fine,
        in_specs=(P(every, None), P(every, None), P(), P(shard, None), P(shard)),
        out_specs=P(shard, "t"),
        check_vma=False,
    )
```

```python
import functools
import math

import jax
import jax.numpy as jnp
from jax import lax
from jax.experimental import pallas as pl
from jax.experimental.pallas import tpu as pltpu
from jax.sharding import Mesh
from jax.sharding import PartitionSpec as P

HEAD = 128
BLOCK = 128
SLOTS = 10
GROUP = 5
KEYS = (SLOTS + 1) * BLOCK
NEG = -1e30
VMEM_LIMIT = 24 * 1024 * 1024
NT = (((1,), (1,)), ((), ()))


def one_hot(hit):
    return jnp.where(hit, 1.0, 0.0).astype(jnp.bfloat16)


def iota(shape, dim):
    return lax.broadcasted_iota(jnp.int32, shape, dim)


def sort_kernel(index_hbm, query_hbm, pairs_hbm, out, index, query, pairs, sems):
    copies = [
        pltpu.make_async_copy(src, dst, sems.at[k])
        for k, (src, dst) in enumerate(((index_hbm, index), (pairs_hbm, pairs), (query_hbm, query)))
    ]
    for copy in copies:
        copy.start()
    z, x, c, t = (lax.axis_index(n) for n in ("z", "x", "c", "t"))
    device = ((z * 4 + x) * 2 + c) * 8 + t
    group = one_hot((iota((64, 256), 1) >> 2) == iota((64, 256), 0))
    copies[0].wait()
    idx = index[...]
    local = jnp.where((idx >> 6) == device, (idx & 63).astype(jnp.float32), 0.0).astype(jnp.bfloat16)
    source = jnp.sum(jnp.dot(group, local, preferred_element_type=jnp.float32), 1, keepdims=True)
    picker = one_hot(source.astype(jnp.int32) == iota((64, 64), 1))
    copies[1].wait()
    copies[2].wait()
    for t in range(8):
        q = jnp.dot(picker, query[:, t * 640 : (t + 1) * 640], preferred_element_type=jnp.float32)
        kv = jnp.dot(picker, pairs[:, t * 256 : (t + 1) * 256], preferred_element_type=jnp.float32)
        for z in range(8):
            out[z * 8 + t, :, :640] = q[z * 8 : (z + 1) * 8].astype(jnp.bfloat16)
            out[z * 8 + t, :, 640:] = kv[z * 8 : (z + 1) * 8].astype(jnp.bfloat16)


def regroup_kernel(landed, ahead, back, mate, keep, parts):
    x, c = lax.axis_index("x"), lax.axis_index("c")
    want, have = iota((128, 128), 0), iota((128, 128), 1)
    turn = one_hot(((want >> 4) == (have & 7)) & ((want & 15) == (have >> 3)))
    for k in range(4):
        rows = slice(k * 16, (k + 1) * 16)
        got = jnp.dot(turn, landed[rows].reshape(128, 896), preferred_element_type=jnp.float32)
        got = got.astype(jnp.bfloat16)
        for shard in range(8):
            piece = got[shard * 16 : (shard + 1) * 16]
            for h in range(GROUP):
                parts[shard, h, rows, :] = piece[:, h * 128 : (h + 1) * 128]
            for e in range(2):
                pair = piece[:, 640 + e * 128 : 768 + e * 128]
                ahead[10 + shard * 2 + e, rows, :] = pair
                back[shard * 2 + e, rows, :] = pair
                mate[shard * 2 + e, rows, :] = pair
    way = 1 - 2 * c

    def part(step, core):
        return parts[((x + step) & 3) * 2 + (c ^ core)]

    ahead[0:5] = part(2, 0)
    ahead[5:10] = part(2, 1)
    ahead[26:31] = part(way, 1)
    ahead[31:36] = part(way, 0)
    back[16:21] = part(-way, 1)
    back[21:26] = part(-way, 0)
    mate[16:21] = part(0, 1)
    keep[...] = part(0, 0)


def arrival(idx, in_tree):
    source = idx >> 6
    behind = ((in_tree >> 1) - (source >> 4)) & 3
    behind = jnp.where((source & 8) != 0, (4 - behind) & 3, behind)
    order = jnp.where(behind == 2, 3, jnp.where(behind == 3, 2, behind))
    other = ((source >> 3) ^ in_tree) & 1
    return (other << 8) | (order << 6) | ((source >> 6) << 3) | (source & 7)


def picker_of(pos_row):
    column = jnp.transpose(jnp.broadcast_to(pos_row.astype(jnp.float32), (128, 128)))
    parts = []
    for k in range(4):
        lane = (lax.broadcasted_iota(jnp.int32, (128, 128), 1) + k * 128).astype(jnp.float32)
        parts.append(jnp.where(column == lane, 1.0, 0.0).astype(jnp.bfloat16))
    return jnp.concatenate(parts, 1)


def attend_kernel(
    ancestors, depth, index, keep, own, near, far, across, mate, first, rest, out,
    keys, values, local_q, kc, vc, scores, probs,
):
    z, in_tree = lax.axis_index("z"), lax.axis_index("x") * 2 + lax.axis_index("c")
    slabs = ((own, 0), (near, 10), (far, 0), (across, 10), (mate, 0), (first, 0), (rest, 0), (rest, 26))
    parts = ((keep, 0), (near, 31), (far, 21), (across, 0), (mate, 16), (first, 16), (rest, 16), (rest, 21))

    def picked(block, raw):
        pick = picker_of(arrival(index[pl.ds(z * 32 + block, 1), :], in_tree))
        return jnp.dot(pick, raw, preferred_element_type=jnp.float32).astype(jnp.bfloat16)

    def place_shard(j, carry):
        raw = jnp.concatenate(
            [jnp.concatenate([r[base + 2 * j + e] for r, base in slabs], 0) for e in range(2)], 1
        )
        for n in range(4):
            got = picked(j * 4 + n, raw)
            keys[j * 4 + n] = got[:, :128]
            values[j * 4 + n] = got[:, 128:]
        return carry

    lax.fori_loop(0, in_tree + 1, place_shard, 0)
    raw = jnp.concatenate(
        [jnp.concatenate([r[base + h] for r, base in parts], 0) for h in range(GROUP)], 1
    )
    for n in range(4):
        got = picked(in_tree * 4 + n, raw)
        for h in range(GROUP):
            local_q[n, h * 128 : (h + 1) * 128, :] = got[:, h * 128 : (h + 1) * 128]
    vc[:, 128:] = jnp.ones((KEYS, 128), jnp.bfloat16)
    factor = math.log2(math.e) / math.sqrt(HEAD)

    def attend(b, carry):
        levels = depth[b]
        for j in range(SLOTS):
            block = ancestors[b, j] - z * 32
            kc[j * 128 : (j + 1) * 128, :] = keys[block]
            vc[j * 128 : (j + 1) * 128, :128] = values[block]
        me = in_tree * 4 + b
        kc[SLOTS * 128 :, :] = keys[me]
        vc[SLOTS * 128 :, :128] = values[me]
        scores[...] = lax.dot_general(local_q[b], kc[...], NT, preferred_element_type=jnp.float32)
        slot = lax.broadcasted_iota(jnp.int32, (1, SLOTS * 128), 1) >> 7
        bias = jnp.where(slot < levels, 0.0, NEG)
        r = lax.broadcasted_iota(jnp.int32, (128, 128), 0)
        n = lax.broadcasted_iota(jnp.int32, (128, 128), 1)
        causal = jnp.where(n <= r, 0.0, NEG)
        for h in range(GROUP):
            rows = slice(h * 128, (h + 1) * 128)
            s0 = scores[rows, : SLOTS * 128] + bias
            s1 = scores[rows, SLOTS * 128 :] + causal
            top = jnp.maximum(jnp.max(s0, 1, keepdims=True), jnp.max(s1, 1, keepdims=True))
            probs[rows, : SLOTS * 128] = jnp.exp2((s0 - top) * factor).astype(jnp.bfloat16)
            probs[rows, SLOTS * 128 :] = jnp.exp2((s1 - top) * factor).astype(jnp.bfloat16)
        acc = jnp.dot(probs[...], vc[...], preferred_element_type=jnp.float32)
        res = (acc[:, :128] / acc[:, 128:]).astype(jnp.bfloat16)
        for h in range(GROUP):
            out[pl.ds(pl.multiple_of(b * 128, 128), 128), h * 128 : (h + 1) * 128] = res[h * 128 : (h + 1) * 128]
        return carry

    lax.fori_loop(0, 4, attend, 0)


SMEM = pl.BlockSpec(memory_space=pltpu.SMEM)
HBM = pl.BlockSpec(memory_space=pltpu.HBM)
VMEM = pl.BlockSpec(memory_space=pltpu.VMEM)


def ring(block, way):
    route = [(x * 2 + c, (x + (way if c == 0 else -way)) % 4 * 2 + c) for x in range(4) for c in range(2)]
    return lax.ppermute(block, ("x", "c"), route)


def swap(block):
    return lax.ppermute(block, "c", [(0, 1), (1, 0)])


def exchange(block, axes):
    return lax.all_to_all(block, axes, split_axis=0, concat_axis=0, tiled=True)


def finish(ancestors, depth, index, *tiles):
    return pl.pallas_call(
        attend_kernel,
        out_shape=jax.ShapeDtypeStruct((512, 640), jnp.bfloat16),
        in_specs=[SMEM] * 2 + [VMEM] * 9,
        out_specs=VMEM,
        scratch_shapes=[
            pltpu.VMEM((32, 128, 128), jnp.bfloat16),
            pltpu.VMEM((32, 128, 128), jnp.bfloat16),
            pltpu.VMEM((4, 640, 128), jnp.bfloat16),
            pltpu.VMEM((KEYS, 128), jnp.bfloat16),
            pltpu.VMEM((KEYS, 256), jnp.bfloat16),
            pltpu.VMEM((640, KEYS), jnp.float32),
            pltpu.VMEM((640, KEYS), jnp.bfloat16),
        ],
        compiler_params=pltpu.CompilerParams(vmem_limit_bytes=VMEM_LIMIT),
        name="tree_attention",
    )(ancestors, depth, index, *tiles)


def body(query_beam, key_value_beam, beam_row_index, ancestors, depth):
    index = beam_row_index.reshape(256, 128)
    bf16 = jnp.bfloat16
    packed = pl.pallas_call(
        sort_kernel,
        out_shape=jax.ShapeDtypeStruct((64, 8, 896), bf16),
        in_specs=[HBM] * 3,
        out_specs=VMEM,
        scratch_shapes=[
            pltpu.VMEM((256, 128), jnp.int32),
            pltpu.VMEM((64, 5120), bf16),
            pltpu.VMEM((64, 2048), bf16),
            pltpu.SemaphoreType.DMA((3,)),
        ],
        name="sort_rows",
    )(index, query_beam, key_value_beam)
    landed = exchange(packed, ("z", "t"))
    params = pltpu.CompilerParams(vmem_limit_bytes=VMEM_LIMIT)
    ahead, back, mate, keep = pl.pallas_call(
        regroup_kernel,
        out_shape=[jax.ShapeDtypeStruct((n, 64, 128), bf16) for n in (36, 26, 21, 5)],
        in_specs=[VMEM],
        out_specs=[VMEM] * 4,
        scratch_shapes=[pltpu.VMEM((8, GROUP, 64, 128), bf16)],
        compiler_params=params,
        name="regroup",
    )(landed)
    near = ring(ahead, 1)
    far = ring(back, -1)
    mate_swapped = swap(mate)
    near, mate_swapped = lax.optimization_barrier((near, mate_swapped))
    across = ring(near[:26], 1)
    first = swap(near[10:31])
    far, first = lax.optimization_barrier((far, first))
    rest = swap(jnp.concatenate([far[:21], across[5:]], 0))
    return finish(ancestors, depth, index, keep, mate, near, far, across, mate_swapped, first, rest)


def solution(mesh):
    fine = Mesh(mesh.devices.reshape(8, 4, 2, 8), ("z", "x", "c", "t"))
    every, shard = ("z", "x", "c", "t"), ("z", "x", "c")
    return jax.shard_map(
        body,
        mesh=fine,
        in_specs=(P(every, None), P(every, None), P(), P(shard, None), P(shard)),
        out_specs=P(shard, "t"),
        check_vma=False,
    )
```

```python
import functools
import math

import jax
import jax.numpy as jnp
from jax import lax
from jax.experimental import pallas as pl
from jax.experimental.pallas import tpu as pltpu
from jax.sharding import Mesh
from jax.sharding import PartitionSpec as P

HEAD = 128
BLOCK = 128
SLOTS = 10
GROUP = 5
DEPTHS = (7, 10)
KEYS = (SLOTS + 1) * BLOCK
NEG = -1e30
VMEM_LIMIT = 32 * 1024 * 1024
NT = (((1,), (1,)), ((), ()))


def one_hot(hit):
    return jnp.where(hit, 1.0, 0.0).astype(jnp.bfloat16)


def iota(shape, dim):
    return lax.broadcasted_iota(jnp.int32, shape, dim)


def sort_kernel(index_hbm, query_hbm, pairs_hbm, out, index, query, pairs, sems):
    copies = [
        pltpu.make_async_copy(src, dst, sems.at[k])
        for k, (src, dst) in enumerate(((index_hbm, index), (pairs_hbm, pairs), (query_hbm, query)))
    ]
    for copy in copies:
        copy.start()
    z, x, c, t = (lax.axis_index(n) for n in ("z", "x", "c", "t"))
    device = ((z * 4 + x) * 2 + c) * 8 + t
    group = one_hot((iota((64, 256), 1) >> 2) == iota((64, 256), 0))
    copies[0].wait()
    idx = index[...]
    local = jnp.where((idx >> 6) == device, (idx & 63).astype(jnp.float32), 0.0).astype(jnp.bfloat16)
    source = jnp.sum(jnp.dot(group, local, preferred_element_type=jnp.float32), 1, keepdims=True)
    picker = one_hot(source.astype(jnp.int32) == iota((64, 64), 1))
    copies[1].wait()
    copies[2].wait()
    for t in range(8):
        q = jnp.dot(picker, query[:, t * 640 : (t + 1) * 640], preferred_element_type=jnp.float32)
        kv = jnp.dot(picker, pairs[:, t * 256 : (t + 1) * 256], preferred_element_type=jnp.float32)
        for z in range(8):
            out[z * 8 + t, :, :640] = q[z * 8 : (z + 1) * 8].astype(jnp.bfloat16)
            out[z * 8 + t, :, 640:] = kv[z * 8 : (z + 1) * 8].astype(jnp.bfloat16)


def regroup_kernel(landed, ahead, back, mate, keep, parts):
    x, c = lax.axis_index("x"), lax.axis_index("c")
    want, have = iota((128, 128), 0), iota((128, 128), 1)
    turn = one_hot(((want >> 4) == (have & 7)) & ((want & 15) == (have >> 3)))
    for k in range(4):
        rows = slice(k * 16, (k + 1) * 16)
        got = jnp.dot(turn, landed[rows].reshape(128, 896), preferred_element_type=jnp.float32)
        got = got.astype(jnp.bfloat16)
        for shard in range(8):
            piece = got[shard * 16 : (shard + 1) * 16]
            for h in range(GROUP):
                parts[shard, h, rows, :] = piece[:, h * 128 : (h + 1) * 128]
            for e in range(2):
                pair = piece[:, 640 + e * 128 : 768 + e * 128]
                ahead[10 + shard * 2 + e, rows, :] = pair
                back[shard * 2 + e, rows, :] = pair
                mate[shard * 2 + e, rows, :] = pair
    way = 1 - 2 * c

    def part(step, core):
        return parts[((x + step) & 3) * 2 + (c ^ core)]

    ahead[0:5] = part(2, 0)
    ahead[5:10] = part(2, 1)
    ahead[26:31] = part(way, 1)
    ahead[31:36] = part(way, 0)
    back[16:21] = part(-way, 1)
    back[21:26] = part(-way, 0)
    mate[16:21] = part(0, 1)
    keep[...] = part(0, 0)


def arrival(idx, in_tree):
    source = idx >> 6
    behind = ((in_tree >> 1) - (source >> 4)) & 3
    behind = jnp.where((source & 8) != 0, (4 - behind) & 3, behind)
    order = jnp.where(behind == 2, 3, jnp.where(behind == 3, 2, behind))
    other = ((source >> 3) ^ in_tree) & 1
    return (other << 8) | (order << 6) | ((source >> 6) << 3) | (source & 7)


def picker_kernel(index, out):
    z, in_tree = lax.axis_index("z"), lax.axis_index("x") * 2 + lax.axis_index("c")

    def block(n, carry):
        places = arrival(index[pl.ds(z * 32 + n, 1), :], in_tree).astype(jnp.float32)
        column = jnp.transpose(jnp.broadcast_to(places, (128, 128)))
        for k in range(4):
            lane = (iota((128, 128), 1) + k * 128).astype(jnp.float32)
            out[n, :, k * 128 : (k + 1) * 128] = one_hot(column == lane)
        return carry

    lax.fori_loop(0, lax.axis_index("x") * 8 + 8, block, 0)


def attend_kernel(
    ancestors, depth, pickers, keep, own, near, far, across, mate, first, rest, out,
    keys, values, local_q, kc, vc, scores, probs,
):
    z, in_tree = lax.axis_index("z"), lax.axis_index("x") * 2 + lax.axis_index("c")
    slabs = ((own, 0), (near, 10), (far, 0), (across, 10), (mate, 0), (first, 0), (rest, 0), (rest, 26))
    parts = ((keep, 0), (near, 31), (far, 21), (across, 0), (mate, 16), (first, 16), (rest, 16), (rest, 21))

    def gathered(tiles, count):
        return jnp.concatenate(
            [jnp.concatenate([r[base + k] for r, base in tiles], 0) for k in range(count)], 1
        )

    def place_chip(chip, carry):
        for core in range(2):
            j = chip * 2 + core
            raw = jnp.concatenate(
                [jnp.concatenate([r[base + 2 * j + e] for r, base in slabs], 0) for e in range(2)], 1
            )
            pick = jnp.concatenate([pickers[j * 4 + n] for n in range(4)], 0)
            got = jnp.dot(pick, raw, preferred_element_type=jnp.float32).astype(jnp.bfloat16)
            for n in range(4):
                keys[j * 4 + n] = got[n * 128 : (n + 1) * 128, :128]
                values[j * 4 + n, :, :128] = got[n * 128 : (n + 1) * 128, 128:]
        return carry

    lax.fori_loop(0, lax.axis_index("x") + 1, place_chip, 0)
    raw = gathered(parts, GROUP)
    for n in range(4):
        pick = pickers[in_tree * 4 + n]
        got = jnp.dot(pick, raw, preferred_element_type=jnp.float32).astype(jnp.bfloat16)
        for h in range(GROUP):
            local_q[n, h * 128 : (h + 1) * 128, :] = got[:, h * 128 : (h + 1) * 128]
    values[:, :, 128:] = jnp.ones((33, 128, 128), jnp.bfloat16)
    values[32] = jnp.zeros((128, 256), jnp.bfloat16)
    keys[32] = jnp.broadcast_to(keys[0].astype(jnp.float32)[:1], (128, 128)).astype(jnp.bfloat16)
    factor = math.log2(math.e) / math.sqrt(HEAD)
    causal = jnp.where(iota((128, 128), 1) <= iota((128, 128), 0), 0.0, NEG)

    def run(slots):
        last, size = slots * 128, slots * 128 + 128

        def score(b):
            levels, me, even = depth[b], in_tree * 4 + b, b % 2
            spare = jnp.where(levels == 0, 32, ancestors[b, 0] - z * 32)
            for j in range(slots):
                seen = j < levels
                block = ancestors[b, j] - z * 32
                kc[even, j * 128 : (j + 1) * 128, :] = keys[jnp.where(seen, block, spare)]
                vc[even, j * 128 : (j + 1) * 128, :] = values[jnp.where(seen, block, 32)]
            kc[even, last:size, :] = keys[me]
            vc[even, last:size, :] = values[me]
            scores[even, :, :size] = lax.dot_general(
                local_q[b], kc[even, :size], NT, preferred_element_type=jnp.float32
            )

        def weigh(b):
            even = b % 2
            for h in range(GROUP):
                rows = slice(h * 128, (h + 1) * 128)
                s0 = scores[even, rows, :last]
                s1 = scores[even, rows, last:size] + causal
                top = jnp.maximum(jnp.max(s0, 1, keepdims=True), jnp.max(s1, 1, keepdims=True))
                probs[even, rows, :last] = jnp.exp2((s0 - top) * factor).astype(jnp.bfloat16)
                probs[even, rows, last:size] = jnp.exp2((s1 - top) * factor).astype(jnp.bfloat16)

        def collect(b):
            acc = jnp.dot(probs[b % 2, :, :size], vc[b % 2, :size], preferred_element_type=jnp.float32)
            res = (acc[:, :128] / acc[:, 128:]).astype(jnp.bfloat16)
            for h in range(GROUP):
                out[b * 128 : (b + 1) * 128, h * 128 : (h + 1) * 128] = res[h * 128 : (h + 1) * 128]

        score(0)
        for b in range(4):
            if b < 3:
                score(b + 1)
            weigh(b)
            collect(b)

    deepest = functools.reduce(jnp.maximum, [depth[b] for b in range(4)])
    low = -1
    for slots in DEPTHS:
        pl.when((deepest > low) & (deepest <= slots))(functools.partial(run, slots))
        low = slots


SMEM = pl.BlockSpec(memory_space=pltpu.SMEM)
HBM = pl.BlockSpec(memory_space=pltpu.HBM)
VMEM = pl.BlockSpec(memory_space=pltpu.VMEM)


def ring(block, way):
    route = [(x * 2 + c, (x + (way if c == 0 else -way)) % 4 * 2 + c) for x in range(4) for c in range(2)]
    return lax.ppermute(block, ("x", "c"), route)


def swap(block):
    return lax.ppermute(block, "c", [(0, 1), (1, 0)])


def exchange(block, axes):
    return lax.all_to_all(block, axes, split_axis=0, concat_axis=0, tiled=True)


def pickers_of(index):
    return pl.pallas_call(
        picker_kernel,
        out_shape=jax.ShapeDtypeStruct((32, 128, 512), jnp.bfloat16),
        in_specs=[VMEM],
        out_specs=VMEM,
        compiler_params=pltpu.CompilerParams(vmem_limit_bytes=VMEM_LIMIT),
        name="pickers",
    )(index)


def finish(ancestors, depth, pickers, *tiles):
    return pl.pallas_call(
        attend_kernel,
        out_shape=jax.ShapeDtypeStruct((512, 640), jnp.bfloat16),
        in_specs=[SMEM] * 2 + [VMEM] * 9,
        out_specs=VMEM,
        scratch_shapes=[
            pltpu.VMEM((33, 128, 128), jnp.bfloat16),
            pltpu.VMEM((33, 128, 256), jnp.bfloat16),
            pltpu.VMEM((4, 640, 128), jnp.bfloat16),
            pltpu.VMEM((2, KEYS, 128), jnp.bfloat16),
            pltpu.VMEM((2, KEYS, 256), jnp.bfloat16),
            pltpu.VMEM((2, 640, KEYS), jnp.float32),
            pltpu.VMEM((2, 640, KEYS), jnp.bfloat16),
        ],
        compiler_params=pltpu.CompilerParams(vmem_limit_bytes=VMEM_LIMIT),
        name="tree_attention",
    )(ancestors, depth, pickers, *tiles)


def body(query_beam, key_value_beam, beam_row_index, ancestors, depth):
    index = beam_row_index.reshape(256, 128)
    bf16 = jnp.bfloat16
    packed = pl.pallas_call(
        sort_kernel,
        out_shape=jax.ShapeDtypeStruct((64, 8, 896), bf16),
        in_specs=[HBM] * 3,
        out_specs=VMEM,
        scratch_shapes=[
            pltpu.VMEM((256, 128), jnp.int32),
            pltpu.VMEM((64, 5120), bf16),
            pltpu.VMEM((64, 2048), bf16),
            pltpu.SemaphoreType.DMA((3,)),
        ],
        name="sort_rows",
    )(index, query_beam, key_value_beam)
    landed = exchange(packed, ("z", "t"))
    params = pltpu.CompilerParams(vmem_limit_bytes=VMEM_LIMIT)
    ahead, back, mate, keep = pl.pallas_call(
        regroup_kernel,
        out_shape=[jax.ShapeDtypeStruct((n, 64, 128), bf16) for n in (36, 26, 21, 5)],
        in_specs=[VMEM],
        out_specs=[VMEM] * 4,
        scratch_shapes=[pltpu.VMEM((8, GROUP, 64, 128), bf16)],
        compiler_params=params,
        name="regroup",
    )(landed)
    index, ahead = lax.optimization_barrier((index, ahead))
    pickers = pickers_of(index)
    near = ring(ahead, 1)
    far = ring(back, -1)
    mate_swapped = swap(mate)
    near, mate_swapped, pickers = lax.optimization_barrier((near, mate_swapped, pickers))
    across = ring(near[:26], 1)
    first = swap(near[10:31])
    far, first = lax.optimization_barrier((far, first))
    rest = swap(jnp.concatenate([far[:21], across[5:]], 0))
    return finish(ancestors, depth, pickers, keep, mate, near, far, across, mate_swapped, first, rest)


def solution(mesh):
    fine = Mesh(mesh.devices.reshape(8, 4, 2, 8), ("z", "x", "c", "t"))
    every, shard = ("z", "x", "c", "t"), ("z", "x", "c")
    return jax.shard_map(
        body,
        mesh=fine,
        in_specs=(P(every, None), P(every, None), P(), P(shard, None), P(shard)),
        out_specs=P(shard, "t"),
        check_vma=False,
    )
```

```python
import functools
import math

import jax
import jax.numpy as jnp
from jax import lax
from jax.experimental import pallas as pl
from jax.experimental.pallas import tpu as pltpu
from jax.sharding import Mesh
from jax.sharding import PartitionSpec as P

HEAD = 128
BLOCK = 128
SLOTS = 10
GROUP = 5
DEPTHS = (7, 10)
KEYS = (SLOTS + 1) * BLOCK
NEG = -1e30
VMEM_LIMIT = 32 * 1024 * 1024
NT = (((1,), (1,)), ((), ()))


def one_hot(hit):
    return jnp.where(hit, 1.0, 0.0).astype(jnp.bfloat16)


def iota(shape, dim):
    return lax.broadcasted_iota(jnp.int32, shape, dim)


def sort_kernel(index_hbm, query_hbm, pairs_hbm, out, index, query, pairs, made, sems, sent):
    copies = [
        pltpu.make_async_copy(src, dst, sems.at[k])
        for k, (src, dst) in enumerate(((index_hbm, index), (pairs_hbm, pairs), (query_hbm, query)))
    ]
    for copy in copies:
        copy.start()
    z, x, c, t = (lax.axis_index(n) for n in ("z", "x", "c", "t"))
    device = ((z * 4 + x) * 2 + c) * 8 + t
    group = one_hot((iota((64, 256), 1) >> 2) == iota((64, 256), 0))
    copies[0].wait()
    idx = index[...]
    local = jnp.where((idx >> 6) == device, (idx & 63).astype(jnp.float32), 0.0).astype(jnp.bfloat16)
    source = jnp.sum(jnp.dot(group, local, preferred_element_type=jnp.float32), 1, keepdims=True)
    picker = one_hot(source.astype(jnp.int32) == iota((64, 64), 1))
    copies[1].wait()
    copies[2].wait()
    leaving = []
    for t in range(8):
        q = jnp.dot(picker, query[:, t * 640 : (t + 1) * 640], preferred_element_type=jnp.float32)
        kv = jnp.dot(picker, pairs[:, t * 256 : (t + 1) * 256], preferred_element_type=jnp.float32)
        for z in range(8):
            made[z, t, :, :640] = q[z * 8 : (z + 1) * 8].astype(jnp.bfloat16)
            made[z, t, :, 640:] = kv[z * 8 : (z + 1) * 8].astype(jnp.bfloat16)
        leaving.append(pltpu.make_async_copy(made.at[:, t], out.at[:, t], sent.at[t]))
        leaving[-1].start()
    for copy in leaving:
        copy.wait()


def regroup_kernel(landed, ahead, back, mate, keep, parts):
    x, c = lax.axis_index("x"), lax.axis_index("c")
    want, have = iota((128, 128), 0), iota((128, 128), 1)
    turn = one_hot(((want >> 4) == (have & 7)) & ((want & 15) == (have >> 3)))
    for k in range(4):
        rows = slice(k * 16, (k + 1) * 16)
        got = jnp.dot(turn, landed[rows].reshape(128, 896), preferred_element_type=jnp.float32)
        got = got.astype(jnp.bfloat16)
        for shard in range(8):
            piece = got[shard * 16 : (shard + 1) * 16]
            for h in range(GROUP):
                parts[shard, h, rows, :] = piece[:, h * 128 : (h + 1) * 128]
            for e in range(2):
                pair = piece[:, 640 + e * 128 : 768 + e * 128]
                ahead[10 + shard * 2 + e, rows, :] = pair
                back[shard * 2 + e, rows, :] = pair
                mate[shard * 2 + e, rows, :] = pair
    way = 1 - 2 * c

    def part(step, core):
        return parts[((x + step) & 3) * 2 + (c ^ core)]

    ahead[0:5] = part(2, 0)
    ahead[5:10] = part(2, 1)
    ahead[26:31] = part(way, 1)
    ahead[31:36] = part(way, 0)
    back[16:21] = part(-way, 1)
    back[21:26] = part(-way, 0)
    mate[16:21] = part(0, 1)
    keep[...] = part(0, 0)


def arrival(idx, in_tree):
    source = idx >> 6
    behind = ((in_tree >> 1) - (source >> 4)) & 3
    behind = jnp.where((source & 8) != 0, (4 - behind) & 3, behind)
    other = ((source >> 3) ^ in_tree) & 1
    order = jnp.where(behind == 0, other * 3, jnp.where(behind == 2, 4 + other * 3, behind - (behind >> 1) + other * 4))
    return (order << 6) | ((source >> 6) << 3) | (source & 7)


def picker_kernel(index, out):
    z, in_tree = lax.axis_index("z"), lax.axis_index("x") * 2 + lax.axis_index("c")

    def block(n, carry):
        places = arrival(index[pl.ds(z * 32 + n, 1), :], in_tree).astype(jnp.float32)
        column = jnp.transpose(jnp.broadcast_to(places, (128, 128)))
        for k in range(4):
            lane = (iota((128, 128), 1) + k * 128).astype(jnp.float32)
            out[n, :, k * 128 : (k + 1) * 128] = one_hot(column == lane)
        return carry

    lax.fori_loop(0, lax.axis_index("x") * 8 + 8, block, 0)


def gathered(tiles, count, start=0):
    return jnp.concatenate(
        [jnp.concatenate([r[base + start + k] for r, base in tiles], 0) for k in range(count)], 1
    )


def early_kernel(pickers, keep, own, near, far, mate, pairs, queries):
    in_tree = lax.axis_index("x") * 2 + lax.axis_index("c")
    slabs, parts = ((own, 0), (near, 10), (far, 0), (mate, 0)), ((keep, 0), (near, 31), (far, 21), (mate, 16))

    def place_chip(chip, carry):
        for core in range(2):
            j = chip * 2 + core
            pick = jnp.concatenate([pickers[j * 4 + n, :, :256] for n in range(4)], 0)
            got = jnp.dot(pick, gathered(slabs, 2, 2 * j), preferred_element_type=jnp.float32)
            pairs[j] = got.astype(jnp.bfloat16)
        return carry

    lax.fori_loop(0, lax.axis_index("x") + 1, place_chip, 0)
    pick = jnp.concatenate([pickers[in_tree * 4 + n, :, :256] for n in range(4)], 0)
    got = jnp.dot(pick, gathered(parts, GROUP), preferred_element_type=jnp.float32)
    queries[...] = got.astype(jnp.bfloat16)


def attend_kernel(
    ancestors_hbm, depth_hbm, pickers, pairs, queries, across, first, second, rest, out_hbm,
    ancestors, depth, keys, values, local_q, kc, vc, scores, probs, out, sems, sent,
):
    tables = [
        pltpu.make_async_copy(ancestors_hbm, ancestors, sems.at[0]),
        pltpu.make_async_copy(depth_hbm, depth, sems.at[1]),
    ]
    for copy in tables:
        copy.start()
    z, in_tree = lax.axis_index("z"), lax.axis_index("x") * 2 + lax.axis_index("c")
    slabs, parts = ((across, 10), (first, 0), (second, 0), (rest, 5)), ((across, 0), (first, 16), (second, 16), (rest, 0))

    def place_chip(chip, carry):
        for core in range(2):
            j = chip * 2 + core
            pick = jnp.concatenate([pickers[j * 4 + n, :, 256:] for n in range(4)], 0)
            got = jnp.dot(pick, gathered(slabs, 2, 2 * j), preferred_element_type=jnp.float32)
            got = (got + pairs[j].astype(jnp.float32)).astype(jnp.bfloat16)
            for n in range(4):
                keys[j * 4 + n] = got[n * 128 : (n + 1) * 128, :128]
                values[j * 4 + n, :, :128] = got[n * 128 : (n + 1) * 128, 128:]
        return carry

    lax.fori_loop(0, lax.axis_index("x") + 1, place_chip, 0)
    raw = gathered(parts, GROUP)
    for n in range(4):
        pick = pickers[in_tree * 4 + n, :, 256:]
        got = jnp.dot(pick, raw, preferred_element_type=jnp.float32)
        got = (got + queries[n * 128 : (n + 1) * 128].astype(jnp.float32)).astype(jnp.bfloat16)
        for h in range(GROUP):
            local_q[n, h * 128 : (h + 1) * 128, :] = got[:, h * 128 : (h + 1) * 128]
    for copy in tables:
        copy.wait()
    values[:, :, 128:] = jnp.ones((33, 128, 128), jnp.bfloat16)
    values[32] = jnp.zeros((128, 256), jnp.bfloat16)
    keys[32] = jnp.broadcast_to(keys[0].astype(jnp.float32)[:1], (128, 128)).astype(jnp.bfloat16)
    factor = math.log2(math.e) / math.sqrt(HEAD)
    causal = jnp.where(iota((128, 128), 1) <= iota((128, 128), 0), 0.0, NEG)

    def leaving(b):
        return pltpu.make_async_copy(out.at[b], out_hbm.at[pl.ds(b * 128, 128)], sent.at[b])

    def run(slots):
        last, size = slots * 128, slots * 128 + 128

        def score(b):
            levels, me, even = depth[b], in_tree * 4 + b, b % 2
            spare = jnp.where(levels == 0, 32, ancestors[b, 0] - z * 32)
            for j in range(slots):
                seen = j < levels
                block = ancestors[b, j] - z * 32
                kc[even, j * 128 : (j + 1) * 128, :] = keys[jnp.where(seen, block, spare)]
                vc[even, j * 128 : (j + 1) * 128, :] = values[jnp.where(seen, block, 32)]
            kc[even, last:size, :] = keys[me]
            vc[even, last:size, :] = values[me]
            scores[even, :, :size] = lax.dot_general(
                local_q[b], kc[even, :size], NT, preferred_element_type=jnp.float32
            )

        def weigh(b):
            even = b % 2
            for h in range(GROUP):
                rows = slice(h * 128, (h + 1) * 128)
                s0 = scores[even, rows, :last]
                s1 = scores[even, rows, last:size] + causal
                top = jnp.maximum(jnp.max(s0, 1, keepdims=True), jnp.max(s1, 1, keepdims=True))
                probs[even, rows, :last] = jnp.exp2((s0 - top) * factor).astype(jnp.bfloat16)
                probs[even, rows, last:size] = jnp.exp2((s1 - top) * factor).astype(jnp.bfloat16)

        def collect(b):
            acc = jnp.dot(probs[b % 2, :, :size], vc[b % 2, :size], preferred_element_type=jnp.float32)
            res = (acc[:, :128] / acc[:, 128:]).astype(jnp.bfloat16)
            for h in range(GROUP):
                out[b, :, h * 128 : (h + 1) * 128] = res[h * 128 : (h + 1) * 128]
            leaving(b).start()

        score(0)
        for b in range(4):
            if b < 3:
                score(b + 1)
            weigh(b)
            collect(b)

    deepest = functools.reduce(jnp.maximum, [depth[b] for b in range(4)])
    low = -1
    for slots in DEPTHS:
        pl.when((deepest > low) & (deepest <= slots))(functools.partial(run, slots))
        low = slots
    for b in range(4):
        leaving(b).wait()


SMEM = pl.BlockSpec(memory_space=pltpu.SMEM)
HBM = pl.BlockSpec(memory_space=pltpu.HBM)
VMEM = pl.BlockSpec(memory_space=pltpu.VMEM)


def ring(block, way):
    route = [(x * 2 + c, (x + (way if c == 0 else -way)) % 4 * 2 + c) for x in range(4) for c in range(2)]
    return lax.ppermute(block, ("x", "c"), route)


def swap(block):
    return lax.ppermute(block, "c", [(0, 1), (1, 0)])


def exchange(block, axes):
    return lax.all_to_all(block, axes, split_axis=0, concat_axis=0, tiled=True)


def pickers_of(index):
    return pl.pallas_call(
        picker_kernel,
        out_shape=jax.ShapeDtypeStruct((32, 128, 512), jnp.bfloat16),
        in_specs=[VMEM],
        out_specs=VMEM,
        compiler_params=pltpu.CompilerParams(vmem_limit_bytes=VMEM_LIMIT),
        name="pickers",
    )(index)


def early(pickers, *tiles):
    return pl.pallas_call(
        early_kernel,
        out_shape=[
            jax.ShapeDtypeStruct((8, 512, 256), jnp.bfloat16),
            jax.ShapeDtypeStruct((512, 640), jnp.bfloat16),
        ],
        in_specs=[VMEM] * 6,
        out_specs=[VMEM] * 2,
        compiler_params=pltpu.CompilerParams(vmem_limit_bytes=VMEM_LIMIT),
        name="place_early",
    )(pickers, *tiles)


def finish(ancestors, depth, pickers, *tiles):
    return pl.pallas_call(
        attend_kernel,
        out_shape=jax.ShapeDtypeStruct((512, 640), jnp.bfloat16),
        in_specs=[HBM] * 2 + [VMEM] * 7,
        out_specs=HBM,
        scratch_shapes=[
            pltpu.SMEM((4, SLOTS), jnp.int32),
            pltpu.SMEM((4,), jnp.int32),
            pltpu.VMEM((33, 128, 128), jnp.bfloat16),
            pltpu.VMEM((33, 128, 256), jnp.bfloat16),
            pltpu.VMEM((4, 640, 128), jnp.bfloat16),
            pltpu.VMEM((2, KEYS, 128), jnp.bfloat16),
            pltpu.VMEM((2, KEYS, 256), jnp.bfloat16),
            pltpu.VMEM((2, 640, KEYS), jnp.float32),
            pltpu.VMEM((2, 640, KEYS), jnp.bfloat16),
            pltpu.VMEM((4, 128, 640), jnp.bfloat16),
            pltpu.SemaphoreType.DMA((2,)),
            pltpu.SemaphoreType.DMA((4,)),
        ],
        compiler_params=pltpu.CompilerParams(vmem_limit_bytes=VMEM_LIMIT),
        name="tree_attention",
    )(ancestors, depth, pickers, *tiles)


def body(query_beam, key_value_beam, beam_row_index, ancestors, depth):
    index = beam_row_index.reshape(256, 128)
    bf16 = jnp.bfloat16
    packed = pl.pallas_call(
        sort_kernel,
        out_shape=jax.ShapeDtypeStruct((8, 8, 8, 896), bf16),
        in_specs=[HBM] * 3,
        out_specs=HBM,
        scratch_shapes=[
            pltpu.VMEM((256, 128), jnp.int32),
            pltpu.VMEM((64, 5120), bf16),
            pltpu.VMEM((64, 2048), bf16),
            pltpu.VMEM((8, 8, 8, 896), bf16),
            pltpu.SemaphoreType.DMA((3,)),
            pltpu.SemaphoreType.DMA((8,)),
        ],
        name="sort_rows",
    )(index, query_beam, key_value_beam)
    landed = exchange(packed.reshape(64, 8, 896), ("z", "t"))
    params = pltpu.CompilerParams(vmem_limit_bytes=VMEM_LIMIT)
    ahead, back, mate, keep = pl.pallas_call(
        regroup_kernel,
        out_shape=[jax.ShapeDtypeStruct((n, 64, 128), bf16) for n in (36, 26, 21, 5)],
        in_specs=[VMEM],
        out_specs=[VMEM] * 4,
        scratch_shapes=[pltpu.VMEM((8, GROUP, 64, 128), bf16)],
        compiler_params=params,
        name="regroup",
    )(landed)
    index, ahead = lax.optimization_barrier((index, ahead))
    pickers = pickers_of(index)
    near = ring(ahead, 1)
    far = ring(back, -1)
    mate_swapped = swap(mate)
    near, mate_swapped, pickers = lax.optimization_barrier((near, mate_swapped, pickers))
    across = ring(near[:26], 1)
    first = swap(near[10:31])
    second = swap(far[:21])
    pairs, queries = early(pickers, keep, mate, near, far, mate_swapped)
    across, second, pairs, queries = lax.optimization_barrier((across, second, pairs, queries))
    rest = swap(across[5:])
    return finish(ancestors, depth, pickers, pairs, queries, across, first, second, rest)


def solution(mesh):
    fine = Mesh(mesh.devices.reshape(8, 4, 2, 8), ("z", "x", "c", "t"))
    every, shard = ("z", "x", "c", "t"), ("z", "x", "c")
    return jax.shard_map(
        body,
        mesh=fine,
        in_specs=(P(every, None), P(every, None), P(), P(shard, None), P(shard)),
        out_specs=P(shard, "t"),
        check_vma=False,
    )
```

```python
import functools
import math

import jax
import jax.numpy as jnp
from jax import lax
from jax.experimental import pallas as pl
from jax.experimental.pallas import tpu as pltpu
from jax.sharding import Mesh
from jax.sharding import PartitionSpec as P

HEAD = 128
BLOCK = 128
SLOTS = 10
GROUP = 5
DEPTHS = (7, 10)
KEYS = (SLOTS + 1) * BLOCK
NEG = -1e30
VMEM_LIMIT = 32 * 1024 * 1024
NT = (((1,), (1,)), ((), ()))


def one_hot(hit):
    return jnp.where(hit, 1.0, 0.0).astype(jnp.bfloat16)


def iota(shape, dim):
    return lax.broadcasted_iota(jnp.int32, shape, dim)


def sort_kernel(index_hbm, query_hbm, pairs_hbm, out, index, query, pairs, made, sems, sent):
    copies = [
        pltpu.make_async_copy(src, dst, sems.at[k])
        for k, (src, dst) in enumerate(((index_hbm, index), (pairs_hbm, pairs), (query_hbm, query)))
    ]
    for copy in copies:
        copy.start()
    z, x, c, t = (lax.axis_index(n) for n in ("z", "x", "c", "t"))
    device = ((z * 4 + x) * 2 + c) * 8 + t
    group = one_hot((iota((64, 256), 1) >> 2) == iota((64, 256), 0))
    copies[0].wait()
    idx = index[...]
    local = jnp.where((idx >> 6) == device, (idx & 63).astype(jnp.float32), 0.0).astype(jnp.bfloat16)
    source = jnp.sum(jnp.dot(group, local, preferred_element_type=jnp.float32), 1, keepdims=True)
    picker = one_hot(source.astype(jnp.int32) == iota((64, 64), 1))
    copies[1].wait()
    copies[2].wait()
    leaving = []
    for t in range(8):
        q = jnp.dot(picker, query[:, t * 640 : (t + 1) * 640], preferred_element_type=jnp.float32)
        kv = jnp.dot(picker, pairs[:, t * 256 : (t + 1) * 256], preferred_element_type=jnp.float32)
        for z in range(8):
            made[z, t, :, :640] = q[z * 8 : (z + 1) * 8].astype(jnp.bfloat16)
            made[z, t, :, 640:] = kv[z * 8 : (z + 1) * 8].astype(jnp.bfloat16)
        leaving.append(pltpu.make_async_copy(made.at[:, t], out.at[:, t], sent.at[t]))
        leaving[-1].start()
    for copy in leaving:
        copy.wait()


def regroup_kernel(landed, ahead, back, late, mate, keep, parts):
    x, c = lax.axis_index("x"), lax.axis_index("c")
    want, have = iota((128, 128), 0), iota((128, 128), 1)
    turn = one_hot(((want >> 4) == (have & 7)) & ((want & 15) == (have >> 3)))
    for k in range(4):
        rows = slice(k * 16, (k + 1) * 16)
        got = jnp.dot(turn, landed[rows].reshape(128, 896), preferred_element_type=jnp.float32)
        got = got.astype(jnp.bfloat16)
        for shard in range(8):
            piece = got[shard * 16 : (shard + 1) * 16]
            for h in range(GROUP):
                parts[shard, h, rows, :] = piece[:, h * 128 : (h + 1) * 128]
            for e in range(2):
                pair = piece[:, 640 + e * 128 : 768 + e * 128]
                ahead[10 + shard * 2 + e, rows, :] = pair
                back[shard * 2 + e, rows, :] = pair
                mate[shard * 2 + e, rows, :] = pair
    way = 1 - 2 * c

    def part(step, core):
        return parts[((x + step) & 3) * 2 + (c ^ core)]

    ahead[0:5] = part(2, 0)
    ahead[5:10] = part(2, 1)
    late[0:5] = part(way, 1)
    late[5:10] = part(way, 0)
    back[16:21] = part(-way, 1)
    back[21:26] = part(-way, 0)
    mate[16:21] = part(0, 1)
    keep[...] = part(0, 0)


def arrival(idx, in_tree):
    source = idx >> 6
    behind = ((in_tree >> 1) - (source >> 4)) & 3
    behind = jnp.where((source & 8) != 0, (4 - behind) & 3, behind)
    other = ((source >> 3) ^ in_tree) & 1
    order = jnp.where(behind == 0, other * 3, jnp.where(behind == 2, 4 + other * 3, behind - (behind >> 1) + other * 4))
    return (order << 6) | ((source >> 6) << 3) | (source & 7)


def picker_kernel(index, out):
    z, x, c = (lax.axis_index(n) for n in ("z", "x", "c"))
    places = arrival(index[pl.ds(z * 32, 32), :], x * 2 + c).astype(jnp.float32)
    columns = jnp.transpose(jnp.concatenate([places, jnp.zeros((96, 128), jnp.float32)], 0))
    lanes = [(iota((128, 128), 1) + k * 128).astype(jnp.float32) for k in range(4)]

    def chip_blocks(chip):
        for n in range(chip * 8, chip * 8 + 8):
            column = jnp.broadcast_to(columns[:, n : n + 1], (128, 128))
            for k in range(4):
                out[n, :, k * 128 : (k + 1) * 128] = one_hot(column == lanes[k])

    for chip in range(4):
        pl.when(chip <= x)(functools.partial(chip_blocks, chip))


def gathered(tiles, count, start=0):
    return jnp.concatenate(
        [jnp.concatenate([r[base + start + k] for r, base in tiles], 0) for k in range(count)], 1
    )


def early_kernel(pickers, own, near, far, mate, pairs):
    slabs = ((own, 0), (near, 10), (far, 0), (mate, 0))

    def place_chip(chip, carry):
        for core in range(2):
            j = chip * 2 + core
            pick = jnp.concatenate([pickers[j * 4 + n, :, :256] for n in range(4)], 0)
            got = jnp.dot(pick, gathered(slabs, 2, 2 * j), preferred_element_type=jnp.float32)
            pairs[j] = got.astype(jnp.bfloat16)
        return carry

    lax.fori_loop(0, lax.axis_index("x") + 1, place_chip, 0)


def attend_kernel(
    ancestors_hbm, depth_hbm, pickers, pairs, keep, far, mate, across, first, second, rest, out_hbm,
    ancestors, depth, keys, values, local_q, kc, vc, scores, probs, out, sems, sent,
):
    tables = [
        pltpu.make_async_copy(ancestors_hbm, ancestors, sems.at[0]),
        pltpu.make_async_copy(depth_hbm, depth, sems.at[1]),
    ]
    for copy in tables:
        copy.start()
    z, in_tree = lax.axis_index("z"), lax.axis_index("x") * 2 + lax.axis_index("c")
    slabs = ((across, 10), (first, 0), (second, 0), (rest, 5))
    parts = ((keep, 0), (across, 31), (far, 21), (mate, 16), (across, 0), (rest, 21), (second, 16), (rest, 0))

    def place_chip(chip, carry):
        for core in range(2):
            j = chip * 2 + core
            pick = jnp.concatenate([pickers[j * 4 + n, :, 256:] for n in range(4)], 0)
            got = jnp.dot(pick, gathered(slabs, 2, 2 * j), preferred_element_type=jnp.float32)
            got = (got + pairs[j].astype(jnp.float32)).astype(jnp.bfloat16)
            for n in range(4):
                keys[j * 4 + n] = got[n * 128 : (n + 1) * 128, :128]
                values[j * 4 + n, :, :128] = got[n * 128 : (n + 1) * 128, 128:]
        return carry

    lax.fori_loop(0, lax.axis_index("x") + 1, place_chip, 0)
    raw = gathered(parts, GROUP)
    for n in range(4):
        got = jnp.dot(pickers[in_tree * 4 + n], raw, preferred_element_type=jnp.float32).astype(jnp.bfloat16)
        for h in range(GROUP):
            local_q[n, h * 128 : (h + 1) * 128, :] = got[:, h * 128 : (h + 1) * 128]
    for copy in tables:
        copy.wait()
    values[:, :, 128:] = jnp.ones((33, 128, 128), jnp.bfloat16)
    values[32] = jnp.zeros((128, 256), jnp.bfloat16)
    keys[32] = jnp.broadcast_to(keys[0].astype(jnp.float32)[:1], (128, 128)).astype(jnp.bfloat16)
    factor = math.log2(math.e) / math.sqrt(HEAD)
    causal = jnp.where(iota((128, 128), 1) <= iota((128, 128), 0), 0.0, NEG)

    def leaving(b):
        return pltpu.make_async_copy(out.at[b], out_hbm.at[pl.ds(b * 128, 128)], sent.at[b])

    def run(slots):
        last, size = slots * 128, slots * 128 + 128

        def score(b):
            levels, me, even = depth[b], in_tree * 4 + b, b % 2
            spare = jnp.where(levels == 0, 32, ancestors[b, 0] - z * 32)
            for j in range(slots):
                seen = j < levels
                block = ancestors[b, j] - z * 32
                kc[even, j * 128 : (j + 1) * 128, :] = keys[jnp.where(seen, block, spare)]
                vc[even, j * 128 : (j + 1) * 128, :] = values[jnp.where(seen, block, 32)]
            kc[even, last:size, :] = keys[me]
            vc[even, last:size, :] = values[me]
            scores[even, :, :size] = lax.dot_general(
                local_q[b], kc[even, :size], NT, preferred_element_type=jnp.float32
            )

        def weigh(b):
            even = b % 2
            for h in range(GROUP):
                rows = slice(h * 128, (h + 1) * 128)
                s0 = scores[even, rows, :last]
                s1 = scores[even, rows, last:size] + causal
                top = jnp.maximum(jnp.max(s0, 1, keepdims=True), jnp.max(s1, 1, keepdims=True))
                probs[even, rows, :last] = jnp.exp2((s0 - top) * factor).astype(jnp.bfloat16)
                probs[even, rows, last:size] = jnp.exp2((s1 - top) * factor).astype(jnp.bfloat16)

        def collect(b):
            acc = jnp.dot(probs[b % 2, :, :size], vc[b % 2, :size], preferred_element_type=jnp.float32)
            res = (acc[:, :128] / acc[:, 128:]).astype(jnp.bfloat16)
            for h in range(GROUP):
                out[b, :, h * 128 : (h + 1) * 128] = res[h * 128 : (h + 1) * 128]
            leaving(b).start()

        score(0)
        for b in range(4):
            if b < 3:
                score(b + 1)
            weigh(b)
            collect(b)

    deepest = functools.reduce(jnp.maximum, [depth[b] for b in range(4)])
    low = -1
    for slots in DEPTHS:
        pl.when((deepest > low) & (deepest <= slots))(functools.partial(run, slots))
        low = slots
    for b in range(4):
        leaving(b).wait()


SMEM = pl.BlockSpec(memory_space=pltpu.SMEM)
HBM = pl.BlockSpec(memory_space=pltpu.HBM)
VMEM = pl.BlockSpec(memory_space=pltpu.VMEM)


def ring(block, way):
    route = [(x * 2 + c, (x + (way if c == 0 else -way)) % 4 * 2 + c) for x in range(4) for c in range(2)]
    return lax.ppermute(block, ("x", "c"), route)


def swap(block):
    return lax.ppermute(block, "c", [(0, 1), (1, 0)])


def exchange(block, axes):
    return lax.all_to_all(block, axes, split_axis=0, concat_axis=0, tiled=True)


def pickers_of(index):
    return pl.pallas_call(
        picker_kernel,
        out_shape=jax.ShapeDtypeStruct((32, 128, 512), jnp.bfloat16),
        in_specs=[VMEM],
        out_specs=VMEM,
        compiler_params=pltpu.CompilerParams(vmem_limit_bytes=VMEM_LIMIT),
        name="pickers",
    )(index)


def early(pickers, *tiles):
    return pl.pallas_call(
        early_kernel,
        out_shape=jax.ShapeDtypeStruct((8, 512, 256), jnp.bfloat16),
        in_specs=[VMEM] * 5,
        out_specs=VMEM,
        compiler_params=pltpu.CompilerParams(vmem_limit_bytes=VMEM_LIMIT),
        name="place_early",
    )(pickers, *tiles)


def finish(ancestors, depth, pickers, *tiles):
    return pl.pallas_call(
        attend_kernel,
        out_shape=jax.ShapeDtypeStruct((512, 640), jnp.bfloat16),
        in_specs=[HBM] * 2 + [VMEM] * 9,
        out_specs=HBM,
        scratch_shapes=[
            pltpu.SMEM((4, SLOTS), jnp.int32),
            pltpu.SMEM((4,), jnp.int32),
            pltpu.VMEM((33, 128, 128), jnp.bfloat16),
            pltpu.VMEM((33, 128, 256), jnp.bfloat16),
            pltpu.VMEM((4, 640, 128), jnp.bfloat16),
            pltpu.VMEM((2, KEYS, 128), jnp.bfloat16),
            pltpu.VMEM((2, KEYS, 256), jnp.bfloat16),
            pltpu.VMEM((2, 640, KEYS), jnp.float32),
            pltpu.VMEM((2, 640, KEYS), jnp.bfloat16),
            pltpu.VMEM((4, 128, 640), jnp.bfloat16),
            pltpu.SemaphoreType.DMA((2,)),
            pltpu.SemaphoreType.DMA((4,)),
        ],
        compiler_params=pltpu.CompilerParams(vmem_limit_bytes=VMEM_LIMIT),
        name="tree_attention",
    )(ancestors, depth, pickers, *tiles)


def body(query_beam, key_value_beam, beam_row_index, ancestors, depth):
    index = beam_row_index.reshape(256, 128)
    bf16 = jnp.bfloat16
    packed = pl.pallas_call(
        sort_kernel,
        out_shape=jax.ShapeDtypeStruct((8, 8, 8, 896), bf16),
        in_specs=[HBM] * 3,
        out_specs=HBM,
        scratch_shapes=[
            pltpu.VMEM((256, 128), jnp.int32),
            pltpu.VMEM((64, 5120), bf16),
            pltpu.VMEM((64, 2048), bf16),
            pltpu.VMEM((8, 8, 8, 896), bf16),
            pltpu.SemaphoreType.DMA((3,)),
            pltpu.SemaphoreType.DMA((8,)),
        ],
        name="sort_rows",
    )(index, query_beam, key_value_beam)
    landed = exchange(packed.reshape(64, 8, 896), ("z", "t"))
    params = pltpu.CompilerParams(vmem_limit_bytes=VMEM_LIMIT)
    ahead, back, late, mate, keep = pl.pallas_call(
        regroup_kernel,
        out_shape=[jax.ShapeDtypeStruct((n, 64, 128), bf16) for n in (26, 26, 10, 21, 5)],
        in_specs=[VMEM],
        out_specs=[VMEM] * 5,
        scratch_shapes=[pltpu.VMEM((8, GROUP, 64, 128), bf16)],
        compiler_params=params,
        name="regroup",
    )(landed)
    index, ahead = lax.optimization_barrier((index, ahead))
    pickers = pickers_of(index)
    near = ring(ahead, 1)
    far = ring(back, -1)
    own, mate = mate, swap(mate)
    near, mate = lax.optimization_barrier((near, mate))
    across = ring(jnp.concatenate([near, late], 0), 1)
    first = swap(near[10:])
    far, pickers = lax.optimization_barrier((far, pickers))
    second = swap(far[:21])
    pairs = early(pickers, own, near, far, mate)
    across, first, second, pairs = lax.optimization_barrier((across, first, second, pairs))
    rest = swap(across[5:31])
    return finish(ancestors, depth, pickers, pairs, keep, far, mate, across, first, second, rest)


def solution(mesh):
    fine = Mesh(mesh.devices.reshape(8, 4, 2, 8), ("z", "x", "c", "t"))
    every, shard = ("z", "x", "c", "t"), ("z", "x", "c")
    return jax.shard_map(
        body,
        mesh=fine,
        in_specs=(P(every, None), P(every, None), P(), P(shard, None), P(shard)),
        out_specs=P(shard, "t"),
        check_vma=False,
    )
```

```python
import functools
import math

import jax
import jax.numpy as jnp
from jax import lax
from jax.experimental import pallas as pl
from jax.experimental.pallas import tpu as pltpu
from jax.sharding import Mesh
from jax.sharding import PartitionSpec as P

HEAD = 128
BLOCK = 128
SLOTS = 10
GROUP = 5
DEPTHS = (7, 10)
KEYS = (SLOTS + 1) * BLOCK
NEG = -1e30
VMEM_LIMIT = 32 * 1024 * 1024
NT = (((1,), (1,)), ((), ()))


def one_hot(hit):
    return jnp.where(hit, 1.0, 0.0).astype(jnp.bfloat16)


def iota(shape, dim):
    return lax.broadcasted_iota(jnp.int32, shape, dim)


def sort_kernel(index_hbm, query_hbm, pairs_hbm, out, index, query, pairs, made, sems, sent):
    copies = [
        pltpu.make_async_copy(src, dst, sems.at[k])
        for k, (src, dst) in enumerate(((index_hbm, index), (pairs_hbm, pairs), (query_hbm, query)))
    ]
    for copy in copies:
        copy.start()
    z, x, c, t = (lax.axis_index(n) for n in ("z", "x", "c", "t"))
    device = ((z * 4 + x) * 2 + c) * 8 + t
    group = one_hot((iota((64, 256), 1) >> 2) == iota((64, 256), 0))
    copies[0].wait()
    idx = index[...]
    local = jnp.where((idx >> 6) == device, (idx & 63).astype(jnp.float32), 0.0).astype(jnp.bfloat16)
    source = jnp.sum(jnp.dot(group, local, preferred_element_type=jnp.float32), 1, keepdims=True)
    picker = one_hot(source.astype(jnp.int32) == iota((64, 64), 1))
    copies[1].wait()
    copies[2].wait()
    leaving = []
    for t in range(8):
        q = jnp.dot(picker, query[:, t * 640 : (t + 1) * 640], preferred_element_type=jnp.float32)
        kv = jnp.dot(picker, pairs[:, t * 256 : (t + 1) * 256], preferred_element_type=jnp.float32)
        for z in range(8):
            made[z, t, :, :640] = q[z * 8 : (z + 1) * 8].astype(jnp.bfloat16)
            made[z, t, :, 640:] = kv[z * 8 : (z + 1) * 8].astype(jnp.bfloat16)
        leaving.append(pltpu.make_async_copy(made.at[:, t], out.at[:, t], sent.at[t]))
        leaving[-1].start()
    for copy in leaving:
        copy.wait()


def regroup_kernel(landed, ahead, back, late, mate, keep, parts):
    x, c = lax.axis_index("x"), lax.axis_index("c")
    want, have = iota((128, 128), 0), iota((128, 128), 1)
    turn = one_hot(((want >> 4) == (have & 7)) & ((want & 15) == (have >> 3)))
    for k in range(4):
        rows = slice(k * 16, (k + 1) * 16)
        got = jnp.dot(turn, landed[rows].reshape(128, 896), preferred_element_type=jnp.float32)
        got = got.astype(jnp.bfloat16)
        for shard in range(8):
            piece = got[shard * 16 : (shard + 1) * 16]
            for h in range(GROUP):
                parts[shard, h, rows, :] = piece[:, h * 128 : (h + 1) * 128]
            for e in range(2):
                pair = piece[:, 640 + e * 128 : 768 + e * 128]
                ahead[10 + shard * 2 + e, rows, :] = pair
                back[shard * 2 + e, rows, :] = pair
                mate[shard * 2 + e, rows, :] = pair
    way = 1 - 2 * c

    def part(step, core):
        return parts[((x + step) & 3) * 2 + (c ^ core)]

    ahead[0:5] = part(2, 0)
    ahead[5:10] = part(2, 1)
    late[0:5] = part(way, 1)
    late[5:10] = part(way, 0)
    back[16:21] = part(-way, 1)
    back[21:26] = part(-way, 0)
    mate[16:21] = part(0, 1)
    keep[...] = part(0, 0)


def arrival(idx, in_tree):
    source = idx >> 6
    behind = ((in_tree >> 1) - (source >> 4)) & 3
    behind = jnp.where((source & 8) != 0, (4 - behind) & 3, behind)
    other = ((source >> 3) ^ in_tree) & 1
    order = jnp.where(behind == 0, other * 3, jnp.where(behind == 2, 4 + other * 3, behind - (behind >> 1) + other * 4))
    return (order << 6) | ((source >> 6) << 3) | (source & 7)


def picker_kernel(index, out):
    z, x, c = (lax.axis_index(n) for n in ("z", "x", "c"))
    places = arrival(index[pl.ds(z * 32, 32), :], x * 2 + c).astype(jnp.float32)
    columns = jnp.transpose(jnp.concatenate([places, jnp.zeros((96, 128), jnp.float32)], 0))
    lanes = [(iota((128, 128), 1) + k * 128).astype(jnp.float32) for k in range(4)]

    def chip_blocks(chip):
        for n in range(chip * 8, chip * 8 + 8):
            column = jnp.broadcast_to(columns[:, n : n + 1], (128, 128))
            for k in range(4):
                out[n, :, k * 128 : (k + 1) * 128] = one_hot(column == lanes[k])

    for chip in range(4):
        pl.when(chip <= x)(functools.partial(chip_blocks, chip))


def gathered(tiles, count, start=0):
    return jnp.concatenate(
        [jnp.concatenate([r[base + start + k] for r, base in tiles], 0) for k in range(count)], 1
    )


def early_kernel(pickers, own, near, far, mate, pairs):
    slabs = ((own, 0), (near, 10), (far, 0), (mate, 0))

    def place_half(half, carry):
        for shard in range(4):
            j = half * 4 + shard
            pick = jnp.concatenate([pickers[j * 4 + n, :, :256] for n in range(4)], 0)
            got = jnp.dot(pick, gathered(slabs, 2, 2 * j), preferred_element_type=jnp.float32)
            pairs[j] = got.astype(jnp.bfloat16)
        return carry

    lax.fori_loop(0, (lax.axis_index("x") + 2) >> 1, place_half, 0)


def attend_kernel(
    ancestors_hbm, depth_hbm, pickers, pairs, keep, far, mate, across, first, second, rest, out_hbm,
    ancestors, depth, keys, values, local_q, kc, vc, scores, probs, out, sems, sent,
):
    tables = [
        pltpu.make_async_copy(ancestors_hbm, ancestors, sems.at[0]),
        pltpu.make_async_copy(depth_hbm, depth, sems.at[1]),
    ]
    for copy in tables:
        copy.start()
    z, in_tree = lax.axis_index("z"), lax.axis_index("x") * 2 + lax.axis_index("c")
    slabs = ((across, 10), (first, 0), (second, 0), (rest, 5))
    parts = ((keep, 0), (across, 31), (far, 21), (mate, 16), (across, 0), (rest, 21), (second, 16), (rest, 0))

    def place_half(half, carry):
        for shard in range(4):
            j = half * 4 + shard
            pick = jnp.concatenate([pickers[j * 4 + n, :, 256:] for n in range(4)], 0)
            got = jnp.dot(pick, gathered(slabs, 2, 2 * j), preferred_element_type=jnp.float32)
            got = (got + pairs[j].astype(jnp.float32)).astype(jnp.bfloat16)
            for n in range(4):
                keys[j * 4 + n] = got[n * 128 : (n + 1) * 128, :128]
                values[j * 4 + n, :, :128] = got[n * 128 : (n + 1) * 128, 128:]
        return carry

    lax.fori_loop(0, (lax.axis_index("x") + 2) >> 1, place_half, 0)
    raw = gathered(parts, GROUP)
    for n in range(4):
        got = jnp.dot(pickers[in_tree * 4 + n], raw, preferred_element_type=jnp.float32).astype(jnp.bfloat16)
        for h in range(GROUP):
            local_q[n, h * 128 : (h + 1) * 128, :] = got[:, h * 128 : (h + 1) * 128]
    for copy in tables:
        copy.wait()
    values[:, :, 128:] = jnp.ones((33, 128, 128), jnp.bfloat16)
    values[32] = jnp.zeros((128, 256), jnp.bfloat16)
    keys[32] = jnp.broadcast_to(keys[0].astype(jnp.float32)[:1], (128, 128)).astype(jnp.bfloat16)
    factor = math.log2(math.e) / math.sqrt(HEAD)
    causal = jnp.where(iota((128, 128), 1) <= iota((128, 128), 0), 0.0, NEG)

    def leaving(b):
        return pltpu.make_async_copy(out.at[b], out_hbm.at[pl.ds(b * 128, 128)], sent.at[b])

    def run(slots):
        last, size = slots * 128, slots * 128 + 128

        def score(b):
            levels, me, even = depth[b], in_tree * 4 + b, b % 2
            spare = jnp.where(levels == 0, 32, ancestors[b, 0] - z * 32)
            for j in range(slots):
                seen = j < levels
                block = ancestors[b, j] - z * 32
                kc[even, j * 128 : (j + 1) * 128, :] = keys[jnp.where(seen, block, spare)]
                vc[even, j * 128 : (j + 1) * 128, :] = values[jnp.where(seen, block, 32)]
            kc[even, last:size, :] = keys[me]
            vc[even, last:size, :] = values[me]
            scores[even, :, :size] = lax.dot_general(
                local_q[b], kc[even, :size], NT, preferred_element_type=jnp.float32
            )

        def weigh(b):
            even = b % 2
            for h in range(GROUP):
                rows = slice(h * 128, (h + 1) * 128)
                s0 = scores[even, rows, :last]
                s1 = scores[even, rows, last:size] + causal
                top = jnp.maximum(jnp.max(s0, 1, keepdims=True), jnp.max(s1, 1, keepdims=True))
                probs[even, rows, :last] = jnp.exp2((s0 - top) * factor).astype(jnp.bfloat16)
                probs[even, rows, last:size] = jnp.exp2((s1 - top) * factor).astype(jnp.bfloat16)

        def collect(b):
            acc = jnp.dot(probs[b % 2, :, :size], vc[b % 2, :size], preferred_element_type=jnp.float32)
            res = (acc[:, :128] / acc[:, 128:]).astype(jnp.bfloat16)
            for h in range(GROUP):
                out[b, :, h * 128 : (h + 1) * 128] = res[h * 128 : (h + 1) * 128]
            leaving(b).start()

        score(0)
        for b in range(4):
            if b < 3:
                score(b + 1)
            weigh(b)
            collect(b)

    deepest = functools.reduce(jnp.maximum, [depth[b] for b in range(4)])
    low = -1
    for slots in DEPTHS:
        pl.when((deepest > low) & (deepest <= slots))(functools.partial(run, slots))
        low = slots
    for b in range(4):
        leaving(b).wait()


SMEM = pl.BlockSpec(memory_space=pltpu.SMEM)
HBM = pl.BlockSpec(memory_space=pltpu.HBM)
VMEM = pl.BlockSpec(memory_space=pltpu.VMEM)


def ring(block, way):
    route = [(x * 2 + c, (x + (way if c == 0 else -way)) % 4 * 2 + c) for x in range(4) for c in range(2)]
    return lax.ppermute(block, ("x", "c"), route)


def swap(block):
    return lax.ppermute(block, "c", [(0, 1), (1, 0)])


def exchange(block, axes):
    return lax.all_to_all(block, axes, split_axis=0, concat_axis=0, tiled=True)


def pickers_of(index):
    return pl.pallas_call(
        picker_kernel,
        out_shape=jax.ShapeDtypeStruct((32, 128, 512), jnp.bfloat16),
        in_specs=[VMEM],
        out_specs=VMEM,
        compiler_params=pltpu.CompilerParams(vmem_limit_bytes=VMEM_LIMIT),
        name="pickers",
    )(index)


def early(pickers, *tiles):
    return pl.pallas_call(
        early_kernel,
        out_shape=jax.ShapeDtypeStruct((8, 512, 256), jnp.bfloat16),
        in_specs=[VMEM] * 5,
        out_specs=VMEM,
        compiler_params=pltpu.CompilerParams(vmem_limit_bytes=VMEM_LIMIT),
        name="place_early",
    )(pickers, *tiles)


def finish(ancestors, depth, pickers, *tiles):
    return pl.pallas_call(
        attend_kernel,
        out_shape=jax.ShapeDtypeStruct((512, 640), jnp.bfloat16),
        in_specs=[HBM] * 2 + [VMEM] * 9,
        out_specs=HBM,
        scratch_shapes=[
            pltpu.SMEM((4, SLOTS), jnp.int32),
            pltpu.SMEM((4,), jnp.int32),
            pltpu.VMEM((33, 128, 128), jnp.bfloat16),
            pltpu.VMEM((33, 128, 256), jnp.bfloat16),
            pltpu.VMEM((4, 640, 128), jnp.bfloat16),
            pltpu.VMEM((2, KEYS, 128), jnp.bfloat16),
            pltpu.VMEM((2, KEYS, 256), jnp.bfloat16),
            pltpu.VMEM((2, 640, KEYS), jnp.float32),
            pltpu.VMEM((2, 640, KEYS), jnp.bfloat16),
            pltpu.VMEM((4, 128, 640), jnp.bfloat16),
            pltpu.SemaphoreType.DMA((2,)),
            pltpu.SemaphoreType.DMA((4,)),
        ],
        compiler_params=pltpu.CompilerParams(vmem_limit_bytes=VMEM_LIMIT),
        name="tree_attention",
    )(ancestors, depth, pickers, *tiles)


def body(query_beam, key_value_beam, beam_row_index, ancestors, depth):
    index = beam_row_index.reshape(256, 128)
    bf16 = jnp.bfloat16
    packed = pl.pallas_call(
        sort_kernel,
        out_shape=jax.ShapeDtypeStruct((8, 8, 8, 896), bf16),
        in_specs=[HBM] * 3,
        out_specs=HBM,
        scratch_shapes=[
            pltpu.VMEM((256, 128), jnp.int32),
            pltpu.VMEM((64, 5120), bf16),
            pltpu.VMEM((64, 2048), bf16),
            pltpu.VMEM((8, 8, 8, 896), bf16),
            pltpu.SemaphoreType.DMA((3,)),
            pltpu.SemaphoreType.DMA((8,)),
        ],
        name="sort_rows",
    )(index, query_beam, key_value_beam)
    landed = exchange(packed.reshape(64, 8, 896), ("z", "t"))
    params = pltpu.CompilerParams(vmem_limit_bytes=VMEM_LIMIT)
    ahead, back, late, mate, keep = pl.pallas_call(
        regroup_kernel,
        out_shape=[jax.ShapeDtypeStruct((n, 64, 128), bf16) for n in (26, 26, 10, 21, 5)],
        in_specs=[VMEM],
        out_specs=[VMEM] * 5,
        scratch_shapes=[pltpu.VMEM((8, GROUP, 64, 128), bf16)],
        compiler_params=params,
        name="regroup",
    )(landed)
    index, ahead = lax.optimization_barrier((index, ahead))
    pickers = pickers_of(index)
    near = ring(ahead, 1)
    far = ring(back, -1)
    own, mate = mate, swap(mate)
    near, mate = lax.optimization_barrier((near, mate))
    across = ring(jnp.concatenate([near, late], 0), 1)
    first = swap(near[10:])
    far, pickers = lax.optimization_barrier((far, pickers))
    second = swap(far[:21])
    pairs = early(pickers, own, near, far, mate)
    across, first, second, pairs = lax.optimization_barrier((across, first, second, pairs))
    rest = swap(across[5:31])
    return finish(ancestors, depth, pickers, pairs, keep, far, mate, across, first, second, rest)


def solution(mesh):
    fine = Mesh(mesh.devices.reshape(8, 4, 2, 8), ("z", "x", "c", "t"))
    every, shard = ("z", "x", "c", "t"), ("z", "x", "c")
    return jax.shard_map(
        body,
        mesh=fine,
        in_specs=(P(every, None), P(every, None), P(), P(shard, None), P(shard)),
        out_specs=P(shard, "t"),
        check_vma=False,
    )
```
